256 devices in a mesh: sector: 16 (over y_lo, x, core), sub: 16 (over z, y_hi).
Axes of the slice: x: 4, y: 4 (y_hi: 2, y_lo: 2; y = y_hi * 2 + y_lo), z: 8, core: 2. Of those that a mesh axis runs over, the one named last changes fastest.
Arguments:
- dual_load: float32 [16, 16, 2, 512, 256], P('sector', 'sub'), may hold values from -50 to 50
- flexibility: bfloat16 [16, 16, 2048, 2048], P('sector', 'sub'), may hold values from -10 to 10, as said below
- face_order: int32 [16, 16, 2048], P('sector', 'sub'), may hold values from 0 to 2047, each once within a row
- corner_index: int32 [16, 16, 32], P('sector', 'sub'), may hold values from 0 to 2047, as said below
- coarse_inverse: float32 [512, 512], replicated, may hold values from -10 to 10, as said below
Outputs:
- multiplier: float32 [16, 16, 2, 512, 256], P('sector', 'sub')
- residual: float32 [16, 16, 2, 512, 256], P('sector', 'sub')
The draws below stay inside these ranges and needn't reach their ends.
Inputs may be any that keep to these rules, and one draw needn't show every extreme that they name: `flexibility`: a block of sizes of order one with a dominant diagonal; each subdomain's matrix is symmetric positive definite. `corner_index`: entries within one subdomain are distinct. `face_order`: each subdomain's row names every face slot once. `coarse_inverse`: symmetric positive definite with a dominant diagonal.
All inputs are finite; a program needn't handle non-finite values.
Results may differ from the reference program's by a relative error of at most 0.0087.
The reference program's roundings to bfloat16 on the way count: a program that leaves them out, or rounds other values in their place, can miss the bound.
Values may be sent and summed in bfloat16 or wider, within the bound.
A program may use at most 128 MiB of HBM per device.

```python
import math
import jax
import jax.numpy as jnp
from jax import lax

NI = 2048
NC = 32
R = 256
ITERS = 2
M = 512
SECTORS = 16
SUBS = 16


def draw_dual_load(key, part):
    first, second = jax.random.split(key, 2)
    shape = (SECTORS, SUBS, 2, M, R)
    position = (jnp.arange(SECTORS)[:, None] * SUBS + jnp.arange(SUBS)[None, :]).astype(jnp.float32)
    factor = 1.0 + 2.0 * position / max(SECTORS * SUBS - 1, 1)
    column = jnp.exp(jax.random.uniform(second, (R,), minval=math.log(0.3), maxval=math.log(3.0)))
    base = jax.random.normal(first, shape)
    values = base * factor[:, :, None, None, None] * column
    return jnp.clip(values, -50.0, 50.0).astype(jnp.float32)


def draw_flexibility(key, part):
    first, second, third = jax.random.split(key, 3)
    shape = (SECTORS, SUBS, NI, NI)
    spread = 0.3 / math.sqrt(NI)
    noise = jax.random.normal(first, shape) * spread
    scales = jnp.exp(jax.random.uniform(second, (SECTORS, SUBS, NI), minval=math.log(0.7), maxval=math.log(1.4)))
    symmetric = (noise + jnp.swapaxes(noise, 2, 3)) / math.sqrt(2.0)
    diagonal = jax.random.uniform(third, (SECTORS, SUBS, NI), minval=1.0, maxval=2.0)
    identity = (jnp.arange(NI)[:, None] == jnp.arange(NI)[None, :]).astype(jnp.float32)
    matrix = symmetric + identity * diagonal[:, :, :, None]
    matrix = matrix * scales[:, :, :, None] * scales[:, :, None, :]
    return jnp.clip(matrix, -10.0, 10.0).astype(jnp.bfloat16)


def draw_corner_index(key, part):
    scores = jax.random.randint(key, (SECTORS, SUBS, NI), 0, 2 ** 19)
    scores = scores * NI + jnp.arange(NI, dtype=jnp.int32)
    ranked = jnp.argsort(scores, axis=-1, stable=True)
    return ranked[:, :, :NC].astype(jnp.int32)


def draw_coarse_inverse(key, part):
    first, second = jax.random.split(jax.random.fold_in(key, 7))
    total = SECTORS * NC
    spread = 0.3 / math.sqrt(total)
    noise = jax.random.normal(first, (total, total)) * spread
    symmetric = (noise + noise.T) / math.sqrt(2.0)
    diagonal = jax.random.uniform(second, (total,), minval=1.0, maxval=2.0)
    identity = (jnp.arange(total)[:, None] == jnp.arange(total)[None, :]).astype(jnp.float32)
    matrix = symmetric + identity * diagonal[:, None]
    return jnp.clip(matrix, -10.0, 10.0).astype(jnp.float32)


def setup_inputs(seed: int = 0) -> dict:
    seeds = jax.random.split(jax.random.key(seed), 6)
    dual_load = draw_dual_load(jax.random.fold_in(seeds[5], 71), 0)
    flexibility = draw_flexibility(jax.random.fold_in(seeds[5], 71), 0)
    face_order = jax.vmap(lambda own: jax.random.permutation(own, NI))(jax.random.split(seeds[2], SECTORS * SUBS)).reshape((SECTORS, SUBS, NI)).astype(jnp.int32)
    corner_index = draw_corner_index(jax.random.fold_in(seeds[5], 71), 0)
    coarse_inverse = draw_coarse_inverse(jax.random.fold_in(seeds[5], 71), 0)
    return {"dual_load": dual_load, "flexibility": flexibility, "face_order": face_order, "corner_index": corner_index, "coarse_inverse": coarse_inverse}


def local_product(operands):
    matrix, slot_order, face_stack = operands
    reordered = jnp.take(jnp.take(matrix, slot_order, axis=0), slot_order, axis=1)
    return jnp.dot(reordered.astype(jnp.float32), face_stack.astype(jnp.float32), precision=lax.Precision.HIGHEST, preferred_element_type=jnp.float32)


def add_corner(target, corner_slots, coarse_add):
    return target.at[corner_slots].add(coarse_add)


def apply_operator(direction, flexibility, face_order, corner_index, coarse_inverse):
    rounded = direction.astype(jnp.bfloat16)
    lam_sub = rounded[:, :, 0]
    lam_cycle = rounded[:, :, 1]
    lower_sub = jnp.concatenate([jnp.zeros_like(lam_sub[:, :1]), lam_sub[:, :-1]], axis=1)
    previous = jnp.roll(lam_cycle, 1, axis=0)
    face_stack = jnp.concatenate([-lower_sub, lam_sub, -previous, lam_cycle], axis=2)
    flat_faces = face_stack.reshape(SECTORS * SUBS, 4 * M, R)
    flat_matrix = flexibility.reshape(SECTORS * SUBS, 4 * M, 4 * M)
    flat_order = face_order.reshape(SECTORS * SUBS, 4 * M)
    product = lax.map(local_product, (flat_matrix, flat_order, flat_faces))
    flat_corner = corner_index.reshape(SECTORS * SUBS, -1)
    partial_value = jnp.take_along_axis(flat_faces, flat_corner[:, :, None], axis=1).astype(jnp.float32)
    sector_corner = jnp.sum(partial_value.reshape(SECTORS, SUBS, NC, R), axis=1)
    stacked = sector_corner.reshape(SECTORS * NC, R)
    coarse = jnp.dot(coarse_inverse, stacked, precision=lax.Precision.HIGHEST, preferred_element_type=jnp.float32) / SUBS
    coarse_add = jnp.repeat(coarse.reshape(SECTORS, NC, R), SUBS, axis=0)
    image_rows = jax.vmap(add_corner)(product, flat_corner, coarse_add).reshape(SECTORS, SUBS, 4, M, R)
    sent = lax.optimization_barrier(image_rows.astype(jnp.bfloat16)).astype(jnp.float32)
    next_lower = jnp.concatenate([sent[:, 1:, 0], jnp.zeros_like(sent[:, :1, 0])], axis=1)
    jump_sub = image_rows[:, :, 1] - next_lower
    jump_cycle = image_rows[:, :, 3] - jnp.roll(sent[:, :, 2], -1, axis=0)
    return jnp.stack([jump_sub, jump_cycle], axis=2)


def reference(dual_load, flexibility, face_order, corner_index, coarse_inverse):
    multiplier = jnp.zeros_like(dual_load)
    residual = dual_load
    direction = dual_load
    norm_now = jnp.sum(residual * residual, axis=(0, 1, 2, 3))
    for iteration in range(ITERS):
        image = apply_operator(direction, flexibility, face_order, corner_index, coarse_inverse)
        alpha = norm_now / jnp.sum(direction * image, axis=(0, 1, 2, 3))
        multiplier = multiplier + alpha * direction
        residual = residual - alpha * image
        if iteration + 1 < ITERS:
            norm_next = jnp.sum(residual * residual, axis=(0, 1, 2, 3))
            direction = residual + (norm_next / norm_now) * direction
            norm_now = norm_next
    return multiplier, residual
```

```python
import functools

import jax
import jax.numpy as jnp
from jax import lax
from jax.experimental import pallas as pl
from jax.experimental.pallas import tpu as pltpu
from jax.sharding import PartitionSpec as P

ITERS = 2
LANES = 128
MESH = pl.DeviceIdType.MESH
BF16 = jnp.bfloat16
F32 = jnp.float32

HALO_SUB, HALO_SEC, BACK_SUB, BACK_SEC, TIP_SUB, TIP_SEC = range(6)
CORNER_SUB, CORNER_SEC, COARSE_SUB, SUM_SUB, SUM_SEC = range(6, 11)
CHANNELS = 11


def dot(a, b):
    return jnp.dot(a, b, preferred_element_type=F32)


def dot_nt(a, b, precision=None):
    return lax.dot_general(
        a, b, (((1,), (1,)), ((), ())), precision=precision, preferred_element_type=F32
    )


def one_hot(condition):
    return jnp.where(condition, 1.0, 0.0).astype(BF16)


def iota(shape, axis):
    return lax.broadcasted_iota(jnp.int32, shape, axis)


def kernel(
    nsec, nsub,
    dual_hbm, matrix_hbm, order_ref, corner_ref, inverse_hbm,
    mult_ref, res_ref,
    matrix, scatter, gather, order_col, direction, rounded, spread, high, low, own, image,
    outgoing, halo_sub, halo_sec, back_sub, back_sec, tip, tip_sub, tip_sec,
    corner_pad, corner_sub, corner_sec, corner_hot, pick_hot, next_sub_hot, next_sec_hot,
    tip_hot, inverse, packed, part_sub, part_out, part_sec, coarse_out, coarse_all,
    sum_out, sum_sub, sum_mid, sum_sec,
    load_sem, index_send, index_recv, send_sem, recv_sem,
):
    rows = matrix.shape[0]
    m = rows // 4
    cases = direction.shape[1]
    nc = corner_ref.shape[1]
    share = cases // nsub
    sec, sub = lax.axis_index("sector"), lax.axis_index("sub")
    sub_next, sub_prev = lax.rem(sub + 1, nsub), lax.rem(sub + nsub - 1, nsub)
    sec_next, sec_prev = lax.rem(sec + 1, nsec), lax.rem(sec + nsec - 1, nsec)
    has_next, has_prev = sub < nsub - 1, sub > 0
    tile = min(256, m)

    barrier = pltpu.get_barrier_semaphore()

    def greet_sub(k, carry):
        pl.semaphore_signal(
            barrier, inc=1, device_id=(sec, lax.rem(sub + k, nsub)), device_id_type=MESH
        )
        return carry

    def greet_sec(k, carry):
        pl.semaphore_signal(
            barrier, inc=1, device_id=(lax.rem(sec + k, nsec), sub), device_id_type=MESH
        )
        return carry

    lax.fori_loop(1, nsub, greet_sub, 0)
    lax.fori_loop(1, nsec, greet_sec, 0)

    load_dual = pltpu.make_async_copy(dual_hbm, direction, load_sem.at[0])
    load_dual.start()
    load_inverse = [
        pltpu.make_async_copy(
            inverse_hbm.at[pl.ds(pl.multiple_of(sec * nc, nc), nc), :],
            inverse.at[pl.ds(q * nc, nc), :],
            load_sem.at[1 + q],
        )
        for q in range(3)
    ]
    for copy in load_inverse:
        copy.start()
    load_matrix = pltpu.make_async_copy(matrix_hbm, matrix, load_sem.at[4])
    load_matrix.start()

    def remote(source, target, it, channel, device):
        return pltpu.make_async_remote_copy(
            src_ref=source,
            dst_ref=target,
            send_sem=send_sem.at[it, channel],
            recv_sem=recv_sem.at[it, channel],
            device_id=device,
            device_id_type=MESH,
        )

    inverse[3 * nc :, :] = jnp.zeros((LANES - 3 * nc, inverse.shape[1]), F32)
    for it in range(ITERS):
        tip_sub[it, nc:, :] = jnp.zeros((LANES - nc, cases), BF16)
        tip_sec[it, nc:, :] = jnp.zeros((LANES - nc, cases), BF16)

        @pl.when(jnp.logical_not(has_prev))
        def _():
            halo_sub[it] = jnp.zeros((m, cases), BF16)

        @pl.when(jnp.logical_not(has_next))
        def _():
            back_sub[it] = jnp.zeros((m, cases), BF16)
            tip_sub[it, :nc, :] = jnp.zeros((nc, cases), BF16)

    corner_pad[...] = jnp.full((8, LANES), -1, jnp.int32)
    corner_pad[0:1, 0:nc] = corner_ref[...]

    @pl.when(jnp.logical_not(has_next))
    def _():
        corner_sub[...] = jnp.full((8, LANES), -1, jnp.int32)

    load_dual.wait()
    rounded[0] = direction[...].astype(BF16)

    pl.semaphore_wait(barrier, nsub - 1 + nsec - 1)

    tell_sub = pltpu.make_async_remote_copy(
        src_ref=corner_pad, dst_ref=corner_sub, send_sem=index_send.at[0],
        recv_sem=index_recv.at[0], device_id=(sec, sub_prev), device_id_type=MESH,
    )
    tell_sec = pltpu.make_async_remote_copy(
        src_ref=corner_pad, dst_ref=corner_sec, send_sem=index_send.at[1],
        recv_sem=index_recv.at[1], device_id=(sec_prev, sub), device_id_type=MESH,
    )
    pl.when(has_prev)(tell_sub.start)
    tell_sec.start()

    def halo_copies(it):
        return (
            remote(rounded.at[it, pl.ds(0, m)], halo_sub.at[it], it, HALO_SUB, (sec, sub_next)),
            remote(rounded.at[it, pl.ds(m, m)], halo_sec.at[it], it, HALO_SEC, (sec_next, sub)),
        )

    def back_copies(it):
        return (
            remote(outgoing.at[it, pl.ds(0, m)], back_sub.at[it], it, BACK_SUB, (sec, sub_prev)),
            remote(outgoing.at[it, pl.ds(m, m)], back_sec.at[it], it, BACK_SEC, (sec_prev, sub)),
        )

    def tip_copies(it):
        head = pl.ds(0, nc)
        return (
            remote(tip.at[it], tip_sub.at[it, head], it, TIP_SUB, (sec, sub_prev)),
            remote(tip.at[it], tip_sec.at[it, head], it, TIP_SEC, (sec_prev, sub)),
        )

    def send_halo(it):
        to_sub, to_sec = halo_copies(it)
        pl.when(has_next)(to_sub.start)
        to_sec.start()

    send_halo(0)

    order_row = order_ref[...]

    def build_scatter(i, carry):
        base = pl.multiple_of(i * tile, tile)
        index = iota((tile, m), 0) + base
        for block in range(4):
            hot = index == order_row[:, block * m : (block + 1) * m]
            value = -1.0 if block in (0, 2) else 1.0
            scatter[pl.ds(base, tile), block * m : (block + 1) * m] = jnp.where(
                hot, value, 0.0
            ).astype(BF16)
        return carry

    lax.fori_loop(0, rows // tile, build_scatter, 0)

    lane = iota((8, LANES), 1)
    mine = corner_pad[...]
    pl.when(has_next)(tell_sub.wait_recv)
    tell_sec.wait_recv()
    above = corner_sub[...]
    beside = corner_sec[...]
    above_rolled = pltpu.roll(above, nc, axis=1)
    beside_rolled = pltpu.roll(beside, 2 * nc, axis=1)
    own_target = jnp.where(
        mine >= 3 * m, mine - 2 * m,
        jnp.where(jnp.logical_and(mine >= m, mine < 2 * m), mine - m, -1),
    )
    above_target = jnp.where(above_rolled < m, above_rolled, -1)
    beside_target = jnp.where(
        jnp.logical_and(beside_rolled >= 2 * m, beside_rolled < 3 * m), beside_rolled - m, -1
    )
    target = jnp.where(
        lane < nc, own_target,
        jnp.where(lane < 2 * nc, above_target, jnp.where(lane < 3 * nc, beside_target, -1)),
    )

    def as_column(row):
        spread_out = jnp.broadcast_to(row.astype(F32), (LANES, LANES))
        return spread_out.T.astype(jnp.int32)

    target_col = as_column(target[0:1])[:, 0:1]
    place = iota((LANES, 2 * m), 1)
    sign = jnp.where(iota((LANES, 2 * m), 0) < nc, 1.0, -1.0)
    pick_hot[...] = jnp.where(place == target_col, sign, 0.0).astype(BF16)

    mine_first = jnp.where(lane < nc, mine, 0)
    triple = (
        mine_first + pltpu.roll(mine_first, nc, axis=1) + pltpu.roll(mine_first, 2 * nc, axis=1)
    )
    triple = jnp.where(lane < 3 * nc, triple, -1)[0:1]
    next_sub_hot[...] = one_hot(iota((m, LANES), 0) == above[0:1])
    next_sec_hot[...] = one_hot(iota((m, LANES), 0) + 2 * m == beside[0:1])

    def pack_corners(it):
        picked = dot(pick_hot[...], rounded[it])
        packed[it] = picked.T.astype(BF16)

        def share_out(k, carry):
            peer = lax.rem(sub + k, nsub)
            remote(
                packed.at[it, pl.ds(pl.multiple_of(peer * share, share), share)],
                part_sub.at[it, sub], it, CORNER_SUB, (sec, peer),
            ).start()
            return carry

        lax.fori_loop(1, nsub, share_out, 0)
        part_sub[it, sub] = packed[it, pl.ds(pl.multiple_of(sub * share, share), share), :]

    def wait_all(ref, sem):
        pltpu.make_async_copy(ref, ref, sem).wait()

    pack_corners(0)

    order_col[...] = jnp.broadcast_to(order_row.astype(F32), (LANES, rows)).T.astype(jnp.int32)

    def build_gather(i, total):
        base = pl.multiple_of(i * tile, tile)
        hot = iota((tile, LANES), 0) + base == triple
        corner_hot[pl.ds(base, tile), :] = one_hot(hot)
        column = order_col[pl.ds(base, tile), :]
        total = total + jnp.sum(jnp.where(hot, column, 0), axis=0, keepdims=True)
        cornered = dot(one_hot(hot), jnp.ones((LANES, LANES), BF16)) > 0.5
        block = base // m
        inner = jnp.logical_or(block == 1, block == 3)
        column = jnp.where(jnp.logical_and(cornered, jnp.logical_not(inner)), -1, column)[:, 0:1]
        gather[pl.ds(base, tile), :] = one_hot(iota((tile, rows), 1) == column)
        return total

    at_corner = lax.fori_loop(
        0, rows // tile, build_gather, jnp.zeros((1, LANES), jnp.int32)
    )
    tip_col = as_column(at_corner)[0:nc, 0:1]
    tip_hot[...] = one_hot(iota((nc, rows), 1) == tip_col)
    for copy in load_inverse:
        copy.wait()

    def gather_corner_sums(it):
        wait_all(part_sub.at[it, pl.ds(0, nsub - 1)], recv_sem.at[it, CORNER_SUB])
        total = part_sub[it, 0].astype(F32)
        for k in range(1, nsub):
            total = total + part_sub[it, k].astype(F32)
        total = total + pltpu.roll(total, LANES - nc, axis=1)
        part_out[it] = total

        def share_out(k, carry):
            remote(
                part_out.at[it], part_sec.at[it, sec], it, CORNER_SEC,
                (lax.rem(sec + k, nsec), sub),
            ).start()
            return carry

        lax.fori_loop(1, nsec, share_out, 0)
        part_sec[it, sec] = total

    def solve_coarse(it):
        wait_all(part_sec.at[it, pl.ds(0, nsec - 1)], recv_sem.at[it, CORNER_SEC])
        per = LANES // nc
        lanes = iota((share, LANES), 1)
        stack = []
        for first in range(0, nsec, per):
            piece = jnp.zeros((share, LANES), F32)
            for q in range(per):
                s = first + q
                a = part_sec[it, s]
                b = part_sec[it, (s - 1) % nsec]
                a = pltpu.roll(a, nc * q, axis=1) if q else a
                shift = (nc * q - 2 * nc) % LANES
                b = pltpu.roll(b, shift, axis=1) if shift else b
                inside = jnp.logical_and(lanes >= nc * q, lanes < nc * (q + 1))
                piece = jnp.where(inside, a + b, piece)
            stack.append(piece)
        corners = jnp.concatenate(stack, axis=1)
        coarse = dot_nt(corners, inverse[...], lax.Precision.HIGHEST) / nsub
        first = coarse.astype(BF16).astype(F32)
        second = (coarse - first).astype(BF16).astype(F32)
        third = coarse - first - second
        split = jnp.where(lanes < nc, first, jnp.where(lanes < 2 * nc, second, third))
        coarse_out[it] = split.astype(BF16)
        here = pl.ds(pl.multiple_of(sub * share, share), share)

        def share_out(k, carry):
            remote(
                coarse_out.at[it], coarse_all.at[it, here], it, COARSE_SUB,
                (sec, lax.rem(sub + k, nsub)),
            ).start()
            return carry

        lax.fori_loop(1, nsub, share_out, 0)
        coarse_all[it, here, :] = coarse_out[it]

    def spread_own(it):
        def body(i, carry):
            at = pl.ds(pl.multiple_of(i * tile, tile), tile)
            value = dot(scatter[at, m : 2 * m], rounded[it, :m, :])
            value += dot(scatter[at, 3 * m :], rounded[it, m:, :])
            spread[at, :] = value.astype(BF16)
            return carry

        lax.fori_loop(0, rows // tile, body, 0)

    def spread_halo(it):
        def body(i, carry):
            at = pl.ds(pl.multiple_of(i * tile, tile), tile)
            value = dot(scatter[at, 2 * m : 3 * m], halo_sec[it])
            value += dot(scatter[at, :m], halo_sub[it])
            spread[at, :] = (spread[at, :].astype(F32) + value).astype(BF16)
            return carry

        lax.fori_loop(0, rows // tile, body, 0)

    def multiply():
        def body(i, carry):
            at = pl.ds(pl.multiple_of(i * tile, tile), tile)
            value = dot(matrix[at, :], spread[...])
            top = value.astype(BF16)
            high[at, :] = top
            low[at, :] = (value - top.astype(F32)).astype(BF16)
            return carry

        lax.fori_loop(0, rows // tile, body, 0)

    def gather_out(it, half):
        def body(i, carry):
            at = pl.multiple_of(i * tile, tile)
            outgoing[it, pl.ds(at + half * m, tile), :] = dot(
                gather[pl.ds(at + 2 * half * m, tile), :], high[...]
            ).astype(BF16)
            return carry

        lax.fori_loop(0, m // tile, body, 0)

    def gather_own(half):
        def body(i, carry):
            at = pl.multiple_of(i * tile, tile)
            hot = gather[pl.ds(at + (2 * half + 1) * m, tile), :]
            own[pl.ds(at + half * m, tile), :] = dot(hot, high[...]) + dot(hot, low[...])
            return carry

        lax.fori_loop(0, m // tile, body, 0)

    def all_sum(it, values):
        pieces = []
        for value in values:
            pieces += [value[:, :LANES], value[:, LANES:]]
        pieces += [jnp.zeros((1, LANES), F32)] * (8 - len(pieces))
        sum_out[it] = jnp.concatenate(pieces, axis=0)

        def to_sub(k, carry):
            remote(
                sum_out.at[it], sum_sub.at[it, sub], it, SUM_SUB, (sec, lax.rem(sub + k, nsub))
            ).start()
            return carry

        lax.fori_loop(1, nsub, to_sub, 0)
        sum_sub[it, sub] = sum_out[it]
        wait_all(sum_sub.at[it, pl.ds(0, nsub - 1)], recv_sem.at[it, SUM_SUB])
        sum_mid[it] = jnp.sum(sum_sub[it], axis=0)

        def to_sec(k, carry):
            remote(
                sum_mid.at[it], sum_sec.at[it, sec], it, SUM_SEC, (lax.rem(sec + k, nsec), sub)
            ).start()
            return carry

        lax.fori_loop(1, nsec, to_sec, 0)
        sum_sec[it, sec] = sum_mid[it]
        wait_all(sum_sec.at[it, pl.ds(0, nsec - 1)], recv_sem.at[it, SUM_SEC])
        total = jnp.sum(sum_sec[it], axis=0)
        return [
            jnp.concatenate([total[2 * i : 2 * i + 1], total[2 * i + 1 : 2 * i + 2]], axis=1)
            for i in range(len(values))
        ]

    norm = None
    for it in range(ITERS):
        spread_own(it)
        gather_corner_sums(it)
        to_sub, to_sec = halo_copies(it)
        to_sec.wait_recv()
        pl.when(has_prev)(to_sub.wait_recv)
        spread_halo(it)
        if it == 0:
            load_matrix.wait()
        multiply()
        solve_coarse(it)
        back_to_sub, back_to_sec = back_copies(it)
        gather_out(it, 0)
        pl.when(has_prev)(back_to_sub.start)
        gather_out(it, 1)
        back_to_sec.start()
        at_tip = dot(tip_hot[...], high[...]) + dot(tip_hot[...], low[...])
        wait_all(
            coarse_all.at[it, pl.ds(0, share * (nsub - 1))], recv_sem.at[it, COARSE_SUB]
        )
        select = jnp.logical_and(
            lax.rem(iota((nc, LANES), 1), nc) == iota((nc, LANES), 0),
            iota((nc, LANES), 1) < 3 * nc,
        )
        tip[it] = (at_tip + dot_nt(one_hot(select), coarse_all[it])).astype(BF16)
        tip_to_sub, tip_to_sec = tip_copies(it)
        pl.when(has_prev)(tip_to_sub.start)
        tip_to_sec.start()
        gather_own(0)
        gather_own(1)
        for half, hot, back, rest, back_copy, tip_copy in (
            (1, next_sec_hot, back_sec, tip_sec, back_to_sec, tip_to_sec),
            (0, next_sub_hot, back_sub, tip_sub, back_to_sub, tip_to_sub),
        ):
            if half:
                back_copy.wait_recv()
                tip_copy.wait_recv()
            else:
                pl.when(has_next)(back_copy.wait_recv)
                pl.when(has_next)(tip_copy.wait_recv)
            at = pl.ds(half * m, m)
            corrected = own[at, :] + dot_nt(
                corner_hot[(2 * half + 1) * m : (2 * half + 2) * m, :], coarse_all[it]
            )
            image[at, :] = corrected - (back[it].astype(F32) + dot(hot[...], rest[it]))
        p, q = direction[...], image[...]
        curvature = jnp.sum(p * q, axis=0, keepdims=True)
        if it == 0:
            square = jnp.sum(q * q, axis=0, keepdims=True)
            start = jnp.sum(p * p, axis=0, keepdims=True)
            norm, curvature, square = all_sum(it, [start, curvature, square])
            alpha = norm / curvature
            new = norm - 2.0 * alpha * curvature + alpha * alpha * square
            beta = new / norm
            norm = new
            p = direction[...]
            residual = p - alpha * image[...]
            mult_ref[...] = alpha * p
            res_ref[...] = residual
            direction[...] = residual + beta * p
            rounded[1] = direction[...].astype(BF16)
            send_halo(1)
            pack_corners(1)
        else:
            (curvature,) = all_sum(it, [curvature])
            alpha = norm / curvature
            mult_ref[...] += alpha * direction[...]
            res_ref[...] -= alpha * image[...]

    pl.when(has_prev)(tell_sub.wait_send)
    tell_sec.wait_send()
    for it in range(ITERS):
        to_sub, to_sec = halo_copies(it)
        pl.when(has_next)(to_sub.wait_send)
        to_sec.wait_send()
        for copies in (back_copies(it), tip_copies(it)):
            pl.when(has_prev)(copies[0].wait_send)
            copies[1].wait_send()
        wait_all(part_sub.at[it, pl.ds(0, nsub - 1)], send_sem.at[it, CORNER_SUB])
        wait_all(part_sec.at[it, pl.ds(0, nsec - 1)], send_sem.at[it, CORNER_SEC])
        wait_all(
            coarse_all.at[it, pl.ds(0, share * (nsub - 1))], send_sem.at[it, COARSE_SUB]
        )
        wait_all(sum_sub.at[it, pl.ds(0, nsub - 1)], send_sem.at[it, SUM_SUB])
        wait_all(sum_sec.at[it, pl.ds(0, nsec - 1)], send_sem.at[it, SUM_SEC])


def shards(nsec, nsub, dual_load, flexibility, face_order, corner_index, coarse_inverse):
    _, _, _, m, cases = dual_load.shape
    rows = 4 * m
    nc = corner_index.shape[-1]
    share = cases // nsub
    any_space = pl.BlockSpec(memory_space=pl.ANY)
    vmem = pl.BlockSpec(memory_space=pltpu.VMEM)
    it = ITERS
    scratch = [
        ((rows, rows), BF16),
        ((rows, rows), BF16),
        ((rows, rows), BF16),
        ((rows, LANES), jnp.int32),
        ((2 * m, cases), F32),
        ((it, 2 * m, cases), BF16),
        ((rows, cases), BF16),
        ((rows, cases), BF16),
        ((rows, cases), BF16),
        ((2 * m, cases), F32),
        ((2 * m, cases), F32),
        ((it, 2 * m, cases), BF16),
        ((it, m, cases), BF16),
        ((it, m, cases), BF16),
        ((it, m, cases), BF16),
        ((it, m, cases), BF16),
        ((it, nc, cases), BF16),
        ((it, LANES, cases), BF16),
        ((it, LANES, cases), BF16),
        ((8, LANES), jnp.int32),
        ((8, LANES), jnp.int32),
        ((8, LANES), jnp.int32),
        ((rows, LANES), BF16),
        ((LANES, 2 * m), BF16),
        ((m, LANES), BF16),
        ((m, LANES), BF16),
        ((nc, rows), BF16),
        ((LANES, nsec * nc), F32),
        ((it, cases, LANES), BF16),
        ((it, nsub, share, LANES), BF16),
        ((it, share, LANES), F32),
        ((it, nsec, share, LANES), F32),
        ((it, share, LANES), BF16),
        ((it, cases, LANES), BF16),
        ((it, 8, LANES), F32),
        ((it, nsub, 8, LANES), F32),
        ((it, 8, LANES), F32),
        ((it, nsec, 8, LANES), F32),
    ]
    dma = pltpu.SemaphoreType.DMA
    out = jax.ShapeDtypeStruct((2 * m, cases), F32)
    multiplier, residual = pl.pallas_call(
        functools.partial(kernel, nsec, nsub),
        out_shape=(out, out),
        in_specs=[any_space, any_space, vmem, vmem, any_space],
        out_specs=(vmem, vmem),
        scratch_shapes=[pltpu.VMEM(shape, dtype) for shape, dtype in scratch]
        + [dma((5,)), dma((2,)), dma((2,)), dma((it, CHANNELS)), dma((it, CHANNELS))],
        compiler_params=pltpu.CompilerParams(
            collective_id=0, has_side_effects=True, vmem_limit_bytes=56 * 1024 * 1024
        ),
        cost_estimate=pl.CostEstimate(
            flops=16 * rows * rows * cases, bytes_accessed=2 * rows * rows, transcendentals=0
        ),
    )(
        dual_load.reshape(2 * m, cases),
        flexibility.reshape(rows, rows),
        face_order.reshape(1, rows),
        corner_index.reshape(1, nc),
        coarse_inverse,
    )
    return multiplier.reshape(dual_load.shape), residual.reshape(dual_load.shape)


def solution(mesh):
    spec = P("sector", "sub", None, None, None)
    return jax.shard_map(
        functools.partial(shards, mesh.shape["sector"], mesh.shape["sub"]),
        mesh=mesh,
        in_specs=(
            spec,
            P("sector", "sub", None, None),
            P("sector", "sub", None),
            P("sector", "sub", None),
            P(),
        ),
        out_specs=(spec, spec),
        check_vma=False,
    )
```

```python
import functools

import jax
import jax.numpy as jnp
from jax import lax
from jax.experimental import pallas as pl
from jax.experimental.pallas import tpu as pltpu
from jax.sharding import PartitionSpec as P

ITERS = 2
LANES = 128
MESH = pl.DeviceIdType.MESH
BF16 = jnp.bfloat16
F32 = jnp.float32

HALO_SUB, HALO_SEC, BACK_SUB, BACK_SEC, TIP_SUB, TIP_SEC = range(6)
CORNER_SUB, CORNER_SEC, COARSE_SUB, SUM_SUB, SUM_SEC = range(6, 11)
CHANNELS = 11


def dot(a, b):
    return jnp.dot(a, b, preferred_element_type=F32)


def dot_nt(a, b, precision=None):
    return lax.dot_general(
        a, b, (((1,), (1,)), ((), ())), precision=precision, preferred_element_type=F32
    )


def one_hot(condition):
    return jnp.where(condition, 1.0, 0.0).astype(BF16)


def iota(shape, axis):
    return lax.broadcasted_iota(jnp.int32, shape, axis)


def kernel(
    nsec, nsub,
    dual_hbm, matrix_hbm, order_ref, corner_ref, inverse_hbm,
    direction_hbm, image_hbm, first_ref, turn_ref, second_ref,
    matrix, scatter, gather, direct, order_col, direction, rounded, spread, high, low, own, image,
    image_short, outgoing, halo_sub, halo_sec, back_sub, back_sec, tip, tip_sub, tip_sec,
    corner_pad, corner_sub, corner_sec, corner_hot, pick_hot, outer_hot, next_sub_hot, next_sec_hot,
    tip_hot, inverse, packed, part_sub, part_out, part_sec, coarse_out, coarse_all,
    sum_out, sum_sub, sum_mid, sum_sec,
    load_sem, store_sem, index_send, index_recv, send_sem, recv_sem,
):
    rows = matrix.shape[0]
    m = rows // 4
    cases = direction.shape[1]
    nc = corner_ref.shape[1]
    share = cases // nsub
    sec, sub = lax.axis_index("sector"), lax.axis_index("sub")
    sub_next, sub_prev = lax.rem(sub + 1, nsub), lax.rem(sub + nsub - 1, nsub)
    sec_next, sec_prev = lax.rem(sec + 1, nsec), lax.rem(sec + nsec - 1, nsec)
    has_next, has_prev = sub < nsub - 1, sub > 0
    tile = min(256, m)
    chunk = min(64, m)

    barrier = pltpu.get_barrier_semaphore()

    def greet_sub(k, carry):
        pl.semaphore_signal(
            barrier, inc=1, device_id=(sec, lax.rem(sub + k, nsub)), device_id_type=MESH
        )
        return carry

    def greet_sec(k, carry):
        pl.semaphore_signal(
            barrier, inc=1, device_id=(lax.rem(sec + k, nsec), sub), device_id_type=MESH
        )
        return carry

    lax.fori_loop(1, nsub, greet_sub, 0)
    lax.fori_loop(1, nsec, greet_sec, 0)

    load_dual = pltpu.make_async_copy(dual_hbm, direction, load_sem.at[0])
    load_dual.start()
    load_matrix = pltpu.make_async_copy(matrix_hbm, matrix, load_sem.at[1])
    load_matrix.start()
    load_inverse = []
    for place, owner in ((0, sec), (1, sec_next)):
        for q in range(3):
            copy = pltpu.make_async_copy(
                inverse_hbm.at[pl.ds(pl.multiple_of(owner * nc, nc), nc), :],
                inverse.at[pl.ds(place * LANES + q * nc, nc), :],
                load_sem.at[2 + place * 3 + q],
            )
            copy.start()
            load_inverse.append(copy)

    def remote(source, target, it, channel, device):
        return pltpu.make_async_remote_copy(
            src_ref=source,
            dst_ref=target,
            send_sem=send_sem.at[it, channel],
            recv_sem=recv_sem.at[it, channel],
            device_id=device,
            device_id_type=MESH,
        )

    def wait_all(ref, sems, it, channel):
        pltpu.make_async_copy(ref, ref, sems.at[it, channel]).wait()

    for place in range(2):
        gap = slice(place * LANES + 3 * nc, (place + 1) * LANES)
        inverse[gap, :] = jnp.zeros((LANES - 3 * nc, inverse.shape[1]), F32)
    for it in range(ITERS):

        @pl.when(jnp.logical_not(has_prev))
        def _():
            halo_sub[it] = jnp.zeros((m, cases), BF16)

        @pl.when(jnp.logical_not(has_next))
        def _():
            back_sub[it] = jnp.zeros((m, cases), BF16)
            tip_sub[it] = jnp.zeros((nc, cases), F32)

    corner_pad[...] = jnp.full((8, LANES), -1, jnp.int32)
    corner_pad[0:1, 0:nc] = corner_ref[...]

    @pl.when(jnp.logical_not(has_next))
    def _():
        corner_sub[...] = jnp.full((8, LANES), -1, jnp.int32)

    order_row = order_ref[...]

    def build_scatter(i, carry):
        base = pl.multiple_of(i * tile, tile)
        index = iota((tile, m), 0) + base
        for block in range(4):
            hot = index == order_row[:, block * m : (block + 1) * m]
            value = -1.0 if block in (0, 2) else 1.0
            scatter[pl.ds(base, tile), block * m : (block + 1) * m] = jnp.where(
                hot, value, 0.0
            ).astype(BF16)
        return carry

    lax.fori_loop(0, rows // tile, build_scatter, 0)

    lane = iota((8, LANES), 1)
    mine = corner_pad[...]
    mine_first = jnp.where(lane < nc, mine, 0)
    triple = (
        mine_first + pltpu.roll(mine_first, nc, axis=1) + pltpu.roll(mine_first, 2 * nc, axis=1)
    )
    triple = jnp.where(lane < 3 * nc, triple, -1)[0:1]
    order_col[...] = jnp.broadcast_to(order_row.astype(F32), (LANES, rows)).T.astype(jnp.int32)

    load_dual.wait()

    def round_load(i, carry):
        at = pl.ds(pl.multiple_of(i * chunk, chunk), chunk)
        rounded[0, at, :] = direction[at, :].astype(BF16)
        return carry

    lax.fori_loop(0, 2 * m // chunk, round_load, 0)

    def build_gather(i, total):
        base = pl.multiple_of(i * tile, tile)
        hot = iota((tile, LANES), 0) + base == triple
        corner_hot[pl.ds(base, tile), :] = one_hot(hot)
        column = order_col[pl.ds(base, tile), :]
        total = total + jnp.sum(jnp.where(hot, column, 0), axis=0, keepdims=True)
        cornered = dot(one_hot(hot), jnp.ones((LANES, LANES), BF16)) > 0.5
        block = base // m
        inner = jnp.logical_or(block == 1, block == 3)
        column = jnp.where(jnp.logical_and(cornered, jnp.logical_not(inner)), -1, column)[:, 0:1]
        gather[pl.ds(base, tile), :] = one_hot(iota((tile, rows), 1) == column)
        return total

    at_corner = lax.fori_loop(
        0, rows // tile, build_gather, jnp.zeros((1, LANES), jnp.int32)
    )

    def as_column(row):
        spread_out = jnp.broadcast_to(row.astype(F32), (LANES, LANES))
        return spread_out.T.astype(jnp.int32)

    tip_col = as_column(at_corner)[0:nc, 0:1]
    tip_hot[...] = one_hot(iota((nc, rows), 1) == tip_col)

    pl.semaphore_wait(barrier, nsub - 1 + nsec - 1)

    tell_sub = pltpu.make_async_remote_copy(
        src_ref=corner_pad, dst_ref=corner_sub, send_sem=index_send.at[0],
        recv_sem=index_recv.at[0], device_id=(sec, sub_prev), device_id_type=MESH,
    )
    tell_sec = pltpu.make_async_remote_copy(
        src_ref=corner_pad, dst_ref=corner_sec, send_sem=index_send.at[1],
        recv_sem=index_recv.at[1], device_id=(sec_prev, sub), device_id_type=MESH,
    )
    pl.when(has_prev)(tell_sub.start)
    tell_sec.start()

    def halo_to_sub_copy(it):
        return remote(rounded.at[it, pl.ds(0, m)], halo_sub.at[it], it, HALO_SUB, (sec, sub_next))

    def halo_to_sec_copy(it):
        return remote(rounded.at[it, pl.ds(m, m)], halo_sec.at[it], it, HALO_SEC, (sec_next, sub))

    def halo_copies(it):
        return halo_to_sub_copy(it), halo_to_sec_copy(it)

    def back_copies(it):
        return (
            remote(outgoing.at[it, pl.ds(0, m)], back_sub.at[it], it, BACK_SUB, (sec, sub_prev)),
            remote(outgoing.at[it, pl.ds(m, m)], back_sec.at[it], it, BACK_SEC, (sec_prev, sub)),
        )

    def tip_copies(it):
        return (
            remote(tip.at[it], tip_sub.at[it], it, TIP_SUB, (sec, sub_prev)),
            remote(tip.at[it], tip_sec.at[it], it, TIP_SEC, (sec_prev, sub)),
        )

    def send_halo(it):
        to_sub, to_sec = halo_copies(it)
        pl.when(has_next)(to_sub.start)
        to_sec.start()

    send_halo(0)

    load_matrix.wait()
    steps = rows // tile

    def build_direct(i, carry):
        at = pl.ds(pl.multiple_of(i * tile, tile), tile)
        direct[:, at] = dot(gather[:m, :], matrix[:, at]).astype(BF16)
        return carry

    lax.fori_loop(0, steps // 2, build_direct, 0)

    pl.when(has_next)(tell_sub.wait_recv)
    tell_sec.wait_recv()
    above = corner_sub[...]
    beside = corner_sec[...]
    above_rolled = pltpu.roll(above, nc, axis=1)
    beside_rolled = pltpu.roll(beside, 2 * nc, axis=1)
    own_target = jnp.where(
        mine >= 3 * m, mine - 2 * m,
        jnp.where(jnp.logical_and(mine >= m, mine < 2 * m), mine - m, -1),
    )
    above_target = jnp.where(above_rolled < m, above_rolled, -1)
    beside_target = jnp.where(
        jnp.logical_and(beside_rolled >= 2 * m, beside_rolled < 3 * m), beside_rolled - m, -1
    )
    target = jnp.where(
        lane < nc, own_target,
        jnp.where(lane < 2 * nc, above_target, jnp.where(lane < 3 * nc, beside_target, -1)),
    )
    target_col = as_column(target[0:1])[:, 0:1]
    place = iota((LANES, 2 * m), 1)
    sign = jnp.where(iota((LANES, 2 * m), 0) < nc, 1.0, -1.0)
    pick_hot[...] = jnp.where(place == target_col, sign, 0.0).astype(BF16)
    outer_target = jnp.where(
        mine < m, mine, jnp.where(jnp.logical_and(mine >= 2 * m, mine < 3 * m), mine - m, -1)
    )
    outer_col = as_column(outer_target[0:1])[0:nc, 0:1]
    outer_hot[...] = jnp.where(iota((nc, 2 * m), 1) == outer_col, -1.0, 0.0).astype(BF16)

    def pack_corners(it, source):
        picked = dot(pick_hot[...], source)
        packed[it] = picked.T.astype(BF16)

        def share_out(k, carry):
            peer = lax.rem(sub + k, nsub)
            remote(
                packed.at[it, pl.ds(pl.multiple_of(peer * share, share), share)],
                part_sub.at[it, sub], it, CORNER_SUB, (sec, peer),
            ).start()
            return carry

        lax.fori_loop(1, nsub, share_out, 0)
        part_sub[it, sub] = packed[it, pl.ds(pl.multiple_of(sub * share, share), share), :]

    pack_corners(0, rounded[0])

    next_sub_hot[...] = one_hot(iota((m, LANES), 0) == above[0:1])
    next_sec_hot[...] = one_hot(iota((m, LANES), 0) + 2 * m == beside[0:1])

    def gather_corner_sums(it):
        wait_all(part_sub.at[it, pl.ds(0, nsub - 1)], recv_sem, it, CORNER_SUB)
        total = part_sub[it, 0].astype(F32)
        for k in range(1, nsub):
            total = total + part_sub[it, k].astype(F32)
        total = total + pltpu.roll(total, LANES - nc, axis=1)
        part_out[it] = total

        def share_out(k, carry):
            remote(
                part_out.at[it], part_sec.at[it, sec], it, CORNER_SEC,
                (lax.rem(sec + k, nsec), sub),
            ).start()
            return carry

        lax.fori_loop(1, nsec, share_out, 0)
        part_sec[it, sec] = total

    def solve_coarse(it):
        wait_all(part_sec.at[it, pl.ds(0, nsec - 1)], recv_sem, it, CORNER_SEC)
        per = LANES // nc
        lanes = iota((share, LANES), 1)
        stack = []
        for first in range(0, nsec, per):
            piece = jnp.zeros((share, LANES), F32)
            for q in range(per):
                s = first + q
                a = part_sec[it, s]
                b = part_sec[it, (s - 1) % nsec]
                a = pltpu.roll(a, nc * q, axis=1) if q else a
                shift = (nc * q - 2 * nc) % LANES
                b = pltpu.roll(b, shift, axis=1) if shift else b
                inside = jnp.logical_and(lanes >= nc * q, lanes < nc * (q + 1))
                piece = jnp.where(inside, a + b, piece)
            stack.append(piece)
        corners = jnp.concatenate(stack, axis=1)
        coarse = dot_nt(corners, inverse[...], lax.Precision.HIGHEST) / nsub
        lanes = lax.rem(iota((share, 2 * LANES), 1), LANES)
        first = coarse.astype(BF16).astype(F32)
        second = (coarse - first).astype(BF16).astype(F32)
        third = coarse - first - second
        split = jnp.where(lanes < nc, first, jnp.where(lanes < 2 * nc, second, third))
        coarse_out[it] = split.astype(BF16)
        here = pl.ds(pl.multiple_of(sub * share, share), share)

        def share_out(k, carry):
            remote(
                coarse_out.at[it], coarse_all.at[it, here], it, COARSE_SUB,
                (sec, lax.rem(sub + k, nsub)),
            ).start()
            return carry

        lax.fori_loop(1, nsub, share_out, 0)
        coarse_all[it, here, :] = coarse_out[it]

    def wait_coarse(it):
        wait_all(coarse_all.at[it, pl.ds(0, share * (nsub - 1))], recv_sem, it, COARSE_SUB)

    def spread_own(it):
        value = dot(scatter[:, m : 2 * m], rounded[it, :m, :])
        value += dot(scatter[:, 3 * m :], rounded[it, m:, :])
        spread[...] = value.astype(BF16)

    def spread_more(block, faces):
        value = dot(scatter[:, block * m : (block + 1) * m], faces)
        spread[...] = (spread[...].astype(F32) + value).astype(BF16)

    def multiply():
        half = rows // 2
        for first in (0, half):
            at = slice(first, first + half)
            value = dot(matrix[at, :], spread[...])
            top = value.astype(BF16)
            high[at, :] = top
            low[at, :] = (value - top.astype(F32)).astype(BF16)

    def all_sum_send(it, values):
        pieces = []
        for value in values:
            pieces += [value[:, :LANES], value[:, LANES:]]
        pieces += [jnp.zeros((1, LANES), F32)] * (8 - len(pieces))
        sum_out[it] = jnp.concatenate(pieces, axis=0)

        def to_sub(k, carry):
            remote(
                sum_out.at[it], sum_sub.at[it, sub], it, SUM_SUB, (sec, lax.rem(sub + k, nsub))
            ).start()
            return carry

        lax.fori_loop(1, nsub, to_sub, 0)
        sum_sub[it, sub] = sum_out[it]

    def all_sum_pass(it):
        wait_all(sum_sub.at[it, pl.ds(0, nsub - 1)], recv_sem, it, SUM_SUB)
        sum_mid[it] = jnp.sum(sum_sub[it], axis=0)

        def to_sec(k, carry):
            remote(
                sum_mid.at[it], sum_sec.at[it, sec], it, SUM_SEC, (lax.rem(sec + k, nsec), sub)
            ).start()
            return carry

        lax.fori_loop(1, nsec, to_sec, 0)
        sum_sec[it, sec] = sum_mid[it]

    def all_sum_get(it, count):
        wait_all(sum_sec.at[it, pl.ds(0, nsec - 1)], recv_sem, it, SUM_SEC)
        total = jnp.sum(sum_sec[it], axis=0)
        return [
            jnp.concatenate([total[2 * i : 2 * i + 1], total[2 * i + 1 : 2 * i + 2]], axis=1)
            for i in range(count)
        ]

    spread_own(0)
    lax.fori_loop(steps // 2, steps, build_direct, 0)
    gather_corner_sums(0)
    for copy in load_inverse:
        copy.wait()

    alpha = beta = norm = None
    select = one_hot(
        jnp.logical_and(
            lax.rem(iota((nc, LANES), 1), nc) == iota((nc, LANES), 0),
            iota((nc, LANES), 1) < 3 * nc,
        )
    )

    def fold(x):
        return jnp.sum(x.reshape(x.shape[0] // 8, 8, cases), axis=0)

    def over_rows(x):
        return jnp.sum(x, axis=0, keepdims=True)

    for it in range(ITERS):
        last = it == ITERS - 1

        def expand(hot, place):
            lanes = slice(place * LANES, (place + 1) * LANES)
            value = dot_nt(hot, coarse_all[0, :, lanes])
            if it == 0:
                return value
            return (1.0 + beta) * value - alpha * dot_nt(hot, coarse_all[1, :, lanes])

        back_to_sub, back_to_sec = back_copies(it)
        tip_to_sub, tip_to_sec = tip_copies(it)
        halo_to_sub, halo_to_sec = halo_copies(it)
        if last:
            spread_own(it)
            solve_coarse(it)
        halo_to_sec.wait_recv()
        spread_more(2, halo_sec[it])
        if last:
            wait_coarse(it)
        pl.when(has_prev)(halo_to_sub.wait_recv)
        spread_more(0, halo_sub[it])
        if not last:
            outgoing[it, :m, :] = dot(direct[...], spread[...]).astype(BF16)
            pl.when(has_prev)(back_to_sub.start)
        multiply()
        at_tip = dot(tip_hot[...], high[...]) + dot(tip_hot[...], low[...])
        tip[it] = at_tip
        if last:
            def weigh(i, total):
                here = pl.ds(pl.multiple_of(i * chunk, chunk), chunk)
                value = high[here, :].astype(F32) + low[here, :].astype(F32)
                return total + fold(spread[here, :].astype(F32) * value)

            p_q = over_rows(
                lax.fori_loop(0, rows // chunk, weigh, jnp.zeros((8, cases), F32))
            )
            faces = dot(outer_hot[:, :m], halo_sub[it]) + dot(outer_hot[:, m:], halo_sec[it])
            faces += dot(pick_hot[:nc, :], rounded[it])
            all_sum_send(it, [p_q + over_rows(faces * expand(select, 0))])
            outgoing[it, :m, :] = dot(gather[:m, :], high[...]).astype(BF16)
            pl.when(has_prev)(back_to_sub.start)
        outgoing[it, m:, :] = dot(gather[2 * m : 3 * m, :], high[...]).astype(BF16)
        back_to_sec.start()
        pl.when(has_prev)(tip_to_sub.start)
        tip_to_sec.start()
        if not last:
            solve_coarse(it)
        for half in (1, 0):
            block = 2 * half + 1
            hot = gather[block * m : (block + 1) * m, :]
            own[half * m : (half + 1) * m, :] = dot(hot, high[...]) + dot(hot, low[...])
        if last:
            all_sum_pass(it)
        else:
            wait_coarse(it)
        p_q = jnp.zeros((8, cases), F32)
        q_q = jnp.zeros((8, cases), F32)
        p_p = jnp.zeros((8, cases), F32)
        for half, hot, back, rest, back_copy, tip_copy in (
            (1, next_sec_hot, back_sec, tip_sec, back_to_sec, tip_to_sec),
            (0, next_sub_hot, back_sub, tip_sub, back_to_sub, tip_to_sub),
        ):
            block = 2 * half + 1
            at = slice(half * m, (half + 1) * m)
            own[at, :] = own[at, :] + expand(corner_hot[block * m : (block + 1) * m, :], 0)
            if half:
                tip_copy.wait_recv()
            else:
                pl.when(has_next)(tip_copy.wait_recv)
            value = (rest[it] + expand(select, half)).astype(BF16)
            value = jnp.concatenate([value, jnp.zeros((LANES - nc, cases), BF16)], axis=0)
            own[at, :] = own[at, :] - dot(hot[...], value)
            if half:
                back_copy.wait_recv()
            else:
                pl.when(has_next)(back_copy.wait_recv)

            def finish(i, sums, half=half, back=back):
                base = pl.multiple_of(i * chunk, chunk)
                here = pl.ds(base + half * m, chunk)
                q = own[here, :] - back[it, pl.ds(base, chunk), :].astype(F32)
                image[here, :] = q
                if last:
                    return sums
                p = direction[here, :]
                image_short[here, :] = q.astype(BF16)
                p_q, q_q, p_p = sums
                return p_q + fold(p * q), q_q + fold(q * q), p_p + fold(p * p)

            p_q, q_q, p_p = lax.fori_loop(0, m // chunk, finish, (p_q, q_q, p_p))
        if not last:
            all_sum_send(it, [over_rows(p_p), over_rows(p_q), over_rows(q_q)])
            pack_corners(1, image_short[...])
            all_sum_pass(it)
            gather_corner_sums(1)
            norm, curvature, square = all_sum_get(it, 3)
            alpha = norm / curvature
            new = norm - 2.0 * alpha * curvature + alpha * alpha * square
            beta = new / norm
            norm = new
            for half in range(2):

                def turn(i, carry, half=half):
                    here = pl.ds(pl.multiple_of(i * chunk + half * m, chunk), chunk)
                    p = direction[here, :]
                    p = p - alpha * image[here, :] + beta * p
                    direction[here, :] = p
                    rounded[1, here, :] = p.astype(BF16)
                    return carry

                lax.fori_loop(0, m // chunk, turn, 0)
                if half:
                    halo_to_sec_copy(1).start()
                else:
                    pl.when(has_next)(halo_to_sub_copy(1).start)
            store_direction = pltpu.make_async_copy(direction, direction_hbm, store_sem.at[0])
            store_direction.start()
        else:
            store_image = pltpu.make_async_copy(image, image_hbm, store_sem.at[1])
            store_image.start()
            (curvature,) = all_sum_get(it, 1)
            first_ref[...] = alpha
            turn_ref[...] = beta
            second_ref[...] = norm / curvature

    store_direction.wait()
    store_image.wait()
    pl.when(has_prev)(tell_sub.wait_send)
    tell_sec.wait_send()
    for it in range(ITERS):
        to_sub, to_sec = halo_copies(it)
        pl.when(has_next)(to_sub.wait_send)
        to_sec.wait_send()
        for copies in (back_copies(it), tip_copies(it)):
            pl.when(has_prev)(copies[0].wait_send)
            copies[1].wait_send()
        wait_all(part_sub.at[it, pl.ds(0, nsub - 1)], send_sem, it, CORNER_SUB)
        wait_all(part_sec.at[it, pl.ds(0, nsec - 1)], send_sem, it, CORNER_SEC)
        wait_all(coarse_all.at[it, pl.ds(0, share * (nsub - 1))], send_sem, it, COARSE_SUB)
        wait_all(sum_sub.at[it, pl.ds(0, nsub - 1)], send_sem, it, SUM_SUB)
        wait_all(sum_sec.at[it, pl.ds(0, nsec - 1)], send_sem, it, SUM_SEC)


def shards(nsec, nsub, dual_load, flexibility, face_order, corner_index, coarse_inverse):
    _, _, _, m, cases = dual_load.shape
    rows = 4 * m
    nc = corner_index.shape[-1]
    share = cases // nsub
    any_space = pl.BlockSpec(memory_space=pl.ANY)
    vmem = pl.BlockSpec(memory_space=pltpu.VMEM)
    it = ITERS
    scratch = [
        ((rows, rows), BF16),
        ((rows, rows), BF16),
        ((rows, rows), BF16),
        ((m, rows), BF16),
        ((rows, LANES), jnp.int32),
        ((2 * m, cases), F32),
        ((it, 2 * m, cases), BF16),
        ((rows, cases), BF16),
        ((rows, cases), BF16),
        ((rows, cases), BF16),
        ((2 * m, cases), F32),
        ((2 * m, cases), F32),
        ((2 * m, cases), BF16),
        ((it, 2 * m, cases), BF16),
        ((it, m, cases), BF16),
        ((it, m, cases), BF16),
        ((it, m, cases), BF16),
        ((it, m, cases), BF16),
        ((it, nc, cases), F32),
        ((it, nc, cases), F32),
        ((it, nc, cases), F32),
        ((8, LANES), jnp.int32),
        ((8, LANES), jnp.int32),
        ((8, LANES), jnp.int32),
        ((rows, LANES), BF16),
        ((LANES, 2 * m), BF16),
        ((nc, 2 * m), BF16),
        ((m, LANES), BF16),
        ((m, LANES), BF16),
        ((nc, rows), BF16),
        ((2 * LANES, nsec * nc), F32),
        ((it, cases, LANES), BF16),
        ((it, nsub, share, LANES), BF16),
        ((it, share, LANES), F32),
        ((it, nsec, share, LANES), F32),
        ((it, share, 2 * LANES), BF16),
        ((it, cases, 2 * LANES), BF16),
        ((it, 8, LANES), F32),
        ((it, nsub, 8, LANES), F32),
        ((it, 8, LANES), F32),
        ((it, nsec, 8, LANES), F32),
    ]
    dma = pltpu.SemaphoreType.DMA
    out = jax.ShapeDtypeStruct((2 * m, cases), F32)
    row = jax.ShapeDtypeStruct((1, cases), F32)
    direction, image, first, turn, second = pl.pallas_call(
        functools.partial(kernel, nsec, nsub),
        out_shape=(out, out, row, row, row),
        in_specs=[any_space, any_space, vmem, vmem, any_space],
        out_specs=(any_space, any_space, vmem, vmem, vmem),
        scratch_shapes=[pltpu.VMEM(shape, dtype) for shape, dtype in scratch]
        + [dma((8,)), dma((2,)), dma((2,)), dma((2,)), dma((it, CHANNELS)), dma((it, CHANNELS))],
        compiler_params=pltpu.CompilerParams(
            collective_id=0, has_side_effects=True, vmem_limit_bytes=56 * 1024 * 1024
        ),
        cost_estimate=pl.CostEstimate(
            flops=16 * rows * rows * cases, bytes_accessed=2 * rows * rows, transcendentals=0
        ),
    )(
        dual_load.reshape(2 * m, cases),
        flexibility.reshape(rows, rows),
        face_order.reshape(1, rows),
        corner_index.reshape(1, nc),
        coarse_inverse,
    )
    direction, image = direction.reshape(dual_load.shape), image.reshape(dual_load.shape)
    first, turn, second = first.reshape(cases), turn.reshape(cases), second.reshape(cases)
    multiplier = first * dual_load + second * direction
    residual = direction - turn * dual_load - second * image
    return multiplier, residual


def solution(mesh):
    spec = P("sector", "sub", None, None, None)
    return jax.shard_map(
        functools.partial(shards, mesh.shape["sector"], mesh.shape["sub"]),
        mesh=mesh,
        in_specs=(
            spec,
            P("sector", "sub", None, None),
            P("sector", "sub", None),
            P("sector", "sub", None),
            P(),
        ),
        out_specs=(spec, spec),
        check_vma=False,
    )
```

```python
import functools

import jax
import jax.numpy as jnp
from jax import lax
from jax.experimental import pallas as pl
from jax.experimental.pallas import tpu as pltpu
from jax.sharding import PartitionSpec as P

ITERS = 2
LANES = 128
MESH = pl.DeviceIdType.MESH
BF16 = jnp.bfloat16
F32 = jnp.float32

HALO_SUB, HALO_SEC, BACK_SUB, BACK_SEC, TIP_SUB, TIP_SEC = range(6)
CORNER_SUB, CORNER_SEC, COARSE_SUB, SUM_FIRST, SUM_SECOND = range(6, 11)
CHANNELS = 11


def dot(a, b):
    return jnp.dot(a, b, preferred_element_type=F32)


def dot_nt(a, b, precision=None):
    return lax.dot_general(
        a, b, (((1,), (1,)), ((), ())), precision=precision, preferred_element_type=F32
    )


def one_hot(condition):
    return jnp.where(condition, 1.0, 0.0).astype(BF16)


def iota(shape, axis):
    return lax.broadcasted_iota(jnp.int32, shape, axis)


def kernel(
    nsec, nsub,
    dual_hbm, matrix_hbm, order_ref, corner_ref, inverse_hbm,
    direction_hbm, image_hbm, first_ref, turn_ref, second_ref,
    matrix, scatter, gather, order_col, direction, rounded, spread, high, low, own, image,
    image_short, outgoing, halo_sub, halo_sec, back_sub, back_sec, tip, tip_sub, tip_sec,
    corner_pad, corner_sub, corner_sec, corner_hot, pick_hot, outer_hot, next_sub_hot, next_sec_hot,
    tip_hot, inverse, packed, part_sub, part_out, part_sec, coarse_out, coarse_all,
    sum_out, sum_first, sum_mid, sum_second,
    load_sem, store_sem, index_send, index_recv, send_sem, recv_sem,
):
    rows = matrix.shape[0]
    m = rows // 4
    cases = direction.shape[1]
    nc = corner_ref.shape[1]
    share = cases // (nsub // 2)
    half_share = share // 2
    sec, sub = lax.axis_index("sector"), lax.axis_index("sub")
    sub_next, sub_prev = lax.rem(sub + 1, nsub), lax.rem(sub + nsub - 1, nsub)
    sec_next, sec_prev = lax.rem(sec + 1, nsec), lax.rem(sec + nsec - 1, nsec)
    has_next, has_prev = sub < nsub - 1, sub > 0
    tile = min(256, m)
    chunk = min(64, m)

    barrier = pltpu.get_barrier_semaphore()

    turns = nsec // 4
    depth = nsub // 2

    def ring(step, size):
        return min(step, size - step)

    def reach(ahead, aside):
        low, across = aside // 2, aside % 2
        over, along = ahead // (2 * turns), ahead // 2 % turns
        return ring(low, depth) + 2 * across + over + ring(along, turns) + 0.5 * (ahead % 2)

    sub_steps = sorted(range(1, nsub), key=lambda k: -reach(0, k))
    sec_steps = sorted(range(1, nsec), key=lambda k: -reach(k, 0))
    z, y_hi = sub // 2, lax.rem(sub, 2)
    y_lo, x, core = sec // (2 * turns), lax.rem(sec // 2, turns), lax.rem(sec, 2)
    first_steps = sorted(
        ((a, b) for a in range(depth) for b in range(2) if a or b),
        key=lambda step: -ring(step[0], depth) - 0.5 * step[1],
    )
    second_steps = sorted(
        (
            (a, b, c) for a in range(2) for b in range(turns) for c in range(2) if a or b or c
        ),
        key=lambda step: -step[0] - ring(step[1], turns) - 2 * step[2],
    )

    def first_peer(step):
        a, b = step
        return (sec + lax.rem(core + b, 2) - core, lax.rem(z + a, depth) * 2 + y_hi)

    def second_peer(step):
        a, b, c = step
        place = lax.rem(y_lo + a, 2) * turns + lax.rem(x + b, turns)
        return (place * 2 + core, z * 2 + lax.rem(y_hi + c, 2))

    first_slot = z * 2 + core
    second_slot = (y_lo * turns + x) * 2 + y_hi
    peers = [(sec, lax.rem(sub + k, nsub)) for k in sub_steps]
    peers += [(lax.rem(sec + k, nsec), sub) for k in sec_steps]
    peers += [first_peer(step) for step in first_steps if step[0] and step[1]]
    peers += [second_peer(step) for step in second_steps if (step[0] or step[1]) and step[2]]
    for peer in peers:
        pl.semaphore_signal(barrier, inc=1, device_id=peer, device_id_type=MESH)

    load_dual = pltpu.make_async_copy(dual_hbm, direction, load_sem.at[0])
    load_dual.start()
    load_matrix = pltpu.make_async_copy(matrix_hbm, matrix, load_sem.at[1])
    load_matrix.start()
    load_inverse = []
    for place, owner in ((0, sec), (1, sec_next)):
        for q in range(3):
            copy = pltpu.make_async_copy(
                inverse_hbm.at[pl.ds(pl.multiple_of(owner * nc, nc), nc), :],
                inverse.at[pl.ds(place * LANES + q * nc, nc), :],
                load_sem.at[2 + place * 3 + q],
            )
            copy.start()
            load_inverse.append(copy)

    def remote(source, target, it, channel, device):
        return pltpu.make_async_remote_copy(
            src_ref=source,
            dst_ref=target,
            send_sem=send_sem.at[it, channel],
            recv_sem=recv_sem.at[it, channel],
            device_id=device,
            device_id_type=MESH,
        )

    def wait_all(ref, sems, it, channel):
        pltpu.make_async_copy(ref, ref, sems.at[it, channel]).wait()

    for place in range(2):
        gap = slice(place * LANES + 3 * nc, (place + 1) * LANES)
        inverse[gap, :] = jnp.zeros((LANES - 3 * nc, inverse.shape[1]), F32)
    for it in range(ITERS):

        @pl.when(jnp.logical_not(has_prev))
        def _():
            halo_sub[it] = jnp.zeros((m, cases), BF16)

        @pl.when(jnp.logical_not(has_next))
        def _():
            back_sub[it] = jnp.zeros((m, cases), BF16)
            tip_sub[it] = jnp.zeros((nc, cases), F32)

    corner_pad[...] = jnp.full((8, LANES), -1, jnp.int32)
    corner_pad[0:1, 0:nc] = corner_ref[...]

    @pl.when(jnp.logical_not(has_next))
    def _():
        corner_sub[...] = jnp.full((8, LANES), -1, jnp.int32)

    order_row = order_ref[...]

    def build_scatter(i, carry):
        base = pl.multiple_of(i * tile, tile)
        index = iota((tile, m), 0) + base
        for block in range(4):
            hot = index == order_row[:, block * m : (block + 1) * m]
            value = -1.0 if block in (0, 2) else 1.0
            scatter[pl.ds(base, tile), block * m : (block + 1) * m] = jnp.where(
                hot, value, 0.0
            ).astype(BF16)
        return carry

    lax.fori_loop(0, rows // tile, build_scatter, 0)

    lane = iota((8, LANES), 1)
    mine = corner_pad[...]
    mine_first = jnp.where(lane < nc, mine, 0)
    triple = (
        mine_first + pltpu.roll(mine_first, nc, axis=1) + pltpu.roll(mine_first, 2 * nc, axis=1)
    )
    triple = jnp.where(lane < 3 * nc, triple, -1)[0:1]
    order_col[...] = jnp.broadcast_to(order_row.astype(F32), (LANES, rows)).T.astype(jnp.int32)

    load_dual.wait()

    def round_load(i, carry):
        at = pl.ds(pl.multiple_of(i * chunk, chunk), chunk)
        rounded[0, at, :] = direction[at, :].astype(BF16)
        return carry

    lax.fori_loop(0, 2 * m // chunk, round_load, 0)

    def build_gather(i, total):
        base = pl.multiple_of(i * tile, tile)
        hot = iota((tile, LANES), 0) + base == triple
        corner_hot[pl.ds(base, tile), :] = one_hot(hot)
        column = order_col[pl.ds(base, tile), :]
        total = total + jnp.sum(jnp.where(hot, column, 0), axis=0, keepdims=True)
        cornered = dot(one_hot(hot), jnp.ones((LANES, LANES), BF16)) > 0.5
        block = base // m
        inner = jnp.logical_or(block == 1, block == 3)
        column = jnp.where(jnp.logical_and(cornered, jnp.logical_not(inner)), -1, column)[:, 0:1]
        gather[pl.ds(base, tile), :] = one_hot(iota((tile, rows), 1) == column)
        return total

    steps = rows // tile
    ahead = steps // 2
    at_corner = lax.fori_loop(0, ahead, build_gather, jnp.zeros((1, LANES), jnp.int32))
    pl.semaphore_wait(barrier, len(peers))

    tell_sub = pltpu.make_async_remote_copy(
        src_ref=corner_pad, dst_ref=corner_sub, send_sem=index_send.at[0],
        recv_sem=index_recv.at[0], device_id=(sec, sub_prev), device_id_type=MESH,
    )
    tell_sec = pltpu.make_async_remote_copy(
        src_ref=corner_pad, dst_ref=corner_sec, send_sem=index_send.at[1],
        recv_sem=index_recv.at[1], device_id=(sec_prev, sub), device_id_type=MESH,
    )
    pl.when(has_prev)(tell_sub.start)
    tell_sec.start()

    def halo_to_sub_copy(it):
        return remote(rounded.at[it, pl.ds(0, m)], halo_sub.at[it], it, HALO_SUB, (sec, sub_next))

    def halo_to_sec_copy(it):
        return remote(rounded.at[it, pl.ds(m, m)], halo_sec.at[it], it, HALO_SEC, (sec_next, sub))

    def halo_copies(it):
        return halo_to_sub_copy(it), halo_to_sec_copy(it)

    def back_copies(it):
        return (
            remote(outgoing.at[it, pl.ds(0, m)], back_sub.at[it], it, BACK_SUB, (sec, sub_prev)),
            remote(outgoing.at[it, pl.ds(m, m)], back_sec.at[it], it, BACK_SEC, (sec_prev, sub)),
        )

    def tip_copies(it):
        return (
            remote(tip.at[it], tip_sub.at[it], it, TIP_SUB, (sec, sub_prev)),
            remote(tip.at[it], tip_sec.at[it], it, TIP_SEC, (sec_prev, sub)),
        )

    def send_halo(it):
        to_sub, to_sec = halo_copies(it)
        pl.when(has_next)(to_sub.start)
        to_sec.start()

    send_halo(0)
    at_corner = lax.fori_loop(ahead, steps, build_gather, at_corner)

    def as_column(row):
        spread_out = jnp.broadcast_to(row.astype(F32), (LANES, LANES))
        return spread_out.T.astype(jnp.int32)

    tip_col = as_column(at_corner)[0:nc, 0:1]
    tip_hot[...] = one_hot(iota((nc, rows), 1) == tip_col)


    def spread_own(it):
        value = dot(scatter[:, m : 2 * m], rounded[it, :m, :])
        value += dot(scatter[:, 3 * m :], rounded[it, m:, :])
        spread[...] = value.astype(BF16)

    spread_own(0)

    pl.when(has_next)(tell_sub.wait_recv)
    tell_sec.wait_recv()
    above = corner_sub[...]
    beside = corner_sec[...]
    above_rolled = pltpu.roll(above, nc, axis=1)
    beside_rolled = pltpu.roll(beside, 2 * nc, axis=1)
    own_target = jnp.where(
        mine >= 3 * m, mine - 2 * m,
        jnp.where(jnp.logical_and(mine >= m, mine < 2 * m), mine - m, -1),
    )
    above_target = jnp.where(above_rolled < m, above_rolled, -1)
    beside_target = jnp.where(
        jnp.logical_and(beside_rolled >= 2 * m, beside_rolled < 3 * m), beside_rolled - m, -1
    )
    target = jnp.where(
        lane < nc, own_target,
        jnp.where(lane < 2 * nc, above_target, jnp.where(lane < 3 * nc, beside_target, -1)),
    )
    target_col = as_column(target[0:1])[:, 0:1]
    place = iota((LANES, 2 * m), 1)
    sign = jnp.where(iota((LANES, 2 * m), 0) < nc, 1.0, -1.0)
    pick_hot[...] = jnp.where(place == target_col, sign, 0.0).astype(BF16)
    outer_target = jnp.where(
        mine < m, mine, jnp.where(jnp.logical_and(mine >= 2 * m, mine < 3 * m), mine - m, -1)
    )
    outer_col = as_column(outer_target[0:1])[0:nc, 0:1]
    outer_hot[...] = jnp.where(iota((nc, 2 * m), 1) == outer_col, -1.0, 0.0).astype(BF16)

    def pack_corners(it, source):
        picked = dot(pick_hot[...], source)
        packed[it] = picked.T.astype(BF16)

        for k in sub_steps:
            peer = lax.rem(sub + k, nsub)
            remote(
                packed.at[it, pl.ds(pl.multiple_of(peer // 2 * share, share), share)],
                part_sub.at[it, sub], it, CORNER_SUB, (sec, peer),
            ).start()
        part_sub[it, sub] = packed[it, pl.ds(pl.multiple_of(z * share, share), share), :]

    pack_corners(0, rounded[0])

    next_sub_hot[...] = one_hot(iota((m, LANES), 0) == above[0:1])
    next_sec_hot[...] = one_hot(iota((m, LANES), 0) + 2 * m == beside[0:1])

    def gather_corner_sums(it):
        wait_all(part_sub.at[it, pl.ds(0, nsub - 1)], recv_sem, it, CORNER_SUB)
        total = part_sub[it, 0].astype(F32)
        for k in range(1, nsub):
            total = total + part_sub[it, k].astype(F32)
        total = total + pltpu.roll(total, LANES - nc, axis=1)
        lanes = iota((half_share, LANES), 1)
        even = lax.rem(lanes // nc, 2) == 0
        total = jnp.where(even, total[:half_share], pltpu.roll(total[half_share:], nc, axis=1))
        part_out[it] = total

        for k in sec_steps:
            remote(
                part_out.at[it], part_sec.at[it, sec], it, CORNER_SEC,
                (lax.rem(sec + k, nsec), sub),
            ).start()
        part_sec[it, sec] = total

    def solve_coarse(it):
        wait_all(part_sec.at[it, pl.ds(0, nsec - 1)], recv_sem, it, CORNER_SEC)
        per = LANES // nc
        lanes = iota((half_share, LANES), 1)

        def turned(value, shift):
            return pltpu.roll(value, shift % LANES, axis=1) if shift % LANES else value

        halves = []
        for half in range(2):
            stack = []
            for first in range(0, nsec, per):
                piece = jnp.zeros((half_share, LANES), F32)
                for q in range(per):
                    s = first + q
                    here = turned(part_sec[it, s], nc * (q - half))
                    before = turned(part_sec[it, (s - 1) % nsec], nc * (q - 2 - half))
                    inside = jnp.logical_and(lanes >= nc * q, lanes < nc * (q + 1))
                    piece = jnp.where(inside, here + before, piece)
                stack.append(piece)
            halves.append(jnp.concatenate(stack, axis=1))
        corners = jnp.concatenate(halves, axis=0)
        coarse = dot_nt(corners, inverse[...], lax.Precision.HIGHEST) / nsub
        lanes = lax.rem(iota((share, 2 * LANES), 1), LANES)
        first = coarse.astype(BF16).astype(F32)
        second = (coarse - first).astype(BF16).astype(F32)
        third = coarse - first - second
        split = jnp.where(lanes < nc, first, jnp.where(lanes < 2 * nc, second, third))
        coarse_out[it] = split.astype(BF16)
        here = pl.ds(pl.multiple_of(z * share, share), share)

        for k in sorted(range(1, depth), key=lambda k: -ring(k, depth)):
            remote(
                coarse_out.at[it], coarse_all.at[it, here], it, COARSE_SUB,
                (sec, lax.rem(z + k, depth) * 2 + y_hi),
            ).start()
        coarse_all[it, here, :] = coarse_out[it]

    def wait_coarse(it):
        wait_all(coarse_all.at[it, pl.ds(0, share * (depth - 1))], recv_sem, it, COARSE_SUB)

    def spread_more(block, faces):
        value = dot(scatter[:, block * m : (block + 1) * m], faces)
        spread[...] = (spread[...].astype(F32) + value).astype(BF16)

    def multiply():
        half = rows // 2
        for first in (0, half):
            at = slice(first, first + half)
            value = dot(matrix[at, :], spread[...])
            top = value.astype(BF16)
            high[at, :] = top
            low[at, :] = (value - top.astype(F32)).astype(BF16)

    def all_sum_send(it, values):
        pieces = []
        for value in values:
            pieces += [value[:, :LANES], value[:, LANES:]]
        pieces += [jnp.zeros((1, LANES), F32)] * (8 - len(pieces))
        sum_out[it] = jnp.concatenate(pieces, axis=0)

        for step in first_steps:
            remote(
                sum_out.at[it], sum_first.at[it, first_slot], it, SUM_FIRST, first_peer(step)
            ).start()
        sum_first[it, first_slot] = sum_out[it]

    def all_sum_pass(it):
        wait_all(sum_first.at[it, pl.ds(0, len(first_steps))], recv_sem, it, SUM_FIRST)
        sum_mid[it] = jnp.sum(sum_first[it], axis=0)
        for step in second_steps:
            remote(
                sum_mid.at[it], sum_second.at[it, second_slot], it, SUM_SECOND, second_peer(step)
            ).start()
        sum_second[it, second_slot] = sum_mid[it]

    def all_sum_get(it, count):
        wait_all(sum_second.at[it, pl.ds(0, len(second_steps))], recv_sem, it, SUM_SECOND)
        total = jnp.sum(sum_second[it], axis=0)
        return [
            jnp.concatenate([total[2 * i : 2 * i + 1], total[2 * i + 1 : 2 * i + 2]], axis=1)
            for i in range(count)
        ]

    for copy in load_inverse:
        copy.wait()

    alpha = beta = norm = None
    select = one_hot(
        jnp.logical_and(
            lax.rem(iota((nc, LANES), 1), nc) == iota((nc, LANES), 0),
            iota((nc, LANES), 1) < 3 * nc,
        )
    )

    def fold(x):
        return jnp.sum(x.reshape(x.shape[0] // 8, 8, cases), axis=0)

    def over_rows(x):
        return jnp.sum(x, axis=0, keepdims=True)

    for it in range(ITERS):
        last = it == ITERS - 1

        def expand(hot, place):
            lanes = slice(place * LANES, (place + 1) * LANES)
            value = dot_nt(hot, coarse_all[0, :, lanes])
            if it == 0:
                return value
            return (1.0 + beta) * value - alpha * dot_nt(hot, coarse_all[1, :, lanes])

        back_to_sub, back_to_sec = back_copies(it)
        tip_to_sub, tip_to_sec = tip_copies(it)
        halo_to_sub, halo_to_sec = halo_copies(it)
        if last:
            spread_own(it)
            solve_coarse(it)
        halo_to_sec.wait_recv()
        spread_more(2, halo_sec[it])
        if last:
            wait_coarse(it)
        pl.when(has_prev)(halo_to_sub.wait_recv)
        spread_more(0, halo_sub[it])
        if not last:
            gather_corner_sums(0)
            load_matrix.wait()
        multiply()
        at_tip = dot(tip_hot[...], high[...]) + dot(tip_hot[...], low[...])
        tip[it] = at_tip
        if last:
            def weigh(i, total):
                here = pl.ds(pl.multiple_of(i * chunk, chunk), chunk)
                value = high[here, :].astype(F32) + low[here, :].astype(F32)
                return total + fold(spread[here, :].astype(F32) * value)

            p_q = over_rows(
                lax.fori_loop(0, rows // chunk, weigh, jnp.zeros((8, cases), F32))
            )
            faces = dot(outer_hot[:, :m], halo_sub[it]) + dot(outer_hot[:, m:], halo_sec[it])
            faces += dot(pick_hot[:nc, :], rounded[it])
            all_sum_send(it, [p_q + over_rows(faces * expand(select, 0))])
        outgoing[it, :m, :] = dot(gather[:m, :], high[...]).astype(BF16)
        pl.when(has_prev)(back_to_sub.start)
        outgoing[it, m:, :] = dot(gather[2 * m : 3 * m, :], high[...]).astype(BF16)
        back_to_sec.start()
        pl.when(has_prev)(tip_to_sub.start)
        tip_to_sec.start()
        if not last:
            solve_coarse(it)
        for half in (1, 0):
            block = 2 * half + 1
            hot = gather[block * m : (block + 1) * m, :]
            own[half * m : (half + 1) * m, :] = dot(hot, high[...]) + dot(hot, low[...])
        if last:
            all_sum_pass(it)
        else:
            wait_coarse(it)
        p_q = jnp.zeros((8, cases), F32)
        q_q = jnp.zeros((8, cases), F32)
        p_p = jnp.zeros((8, cases), F32)
        for half, hot, back, rest, back_copy, tip_copy in (
            (1, next_sec_hot, back_sec, tip_sec, back_to_sec, tip_to_sec),
            (0, next_sub_hot, back_sub, tip_sub, back_to_sub, tip_to_sub),
        ):
            block = 2 * half + 1
            at = slice(half * m, (half + 1) * m)
            own[at, :] = own[at, :] + expand(corner_hot[block * m : (block + 1) * m, :], 0)
            if half:
                tip_copy.wait_recv()
            else:
                pl.when(has_next)(tip_copy.wait_recv)
            value = (rest[it] + expand(select, half)).astype(BF16)
            value = jnp.concatenate([value, jnp.zeros((LANES - nc, cases), BF16)], axis=0)
            own[at, :] = own[at, :] - dot(hot[...], value)
            if half:
                back_copy.wait_recv()
            else:
                pl.when(has_next)(back_copy.wait_recv)

            def finish(i, sums, half=half, back=back):
                base = pl.multiple_of(i * chunk, chunk)
                here = pl.ds(base + half * m, chunk)
                q = own[here, :] - back[it, pl.ds(base, chunk), :].astype(F32)
                image[here, :] = q
                if last:
                    return sums
                p = direction[here, :]
                image_short[here, :] = q.astype(BF16)
                p_q, q_q, p_p = sums
                return p_q + fold(p * q), q_q + fold(q * q), p_p + fold(p * p)

            p_q, q_q, p_p = lax.fori_loop(0, m // chunk, finish, (p_q, q_q, p_p))
        if not last:
            all_sum_send(it, [over_rows(p_p), over_rows(p_q), over_rows(q_q)])
            pack_corners(1, image_short[...])
            all_sum_pass(it)
            gather_corner_sums(1)
            norm, curvature, square = all_sum_get(it, 3)
            alpha = norm / curvature
            new = norm - 2.0 * alpha * curvature + alpha * alpha * square
            beta = new / norm
            norm = new
            for half in range(2):

                def turn(i, carry, half=half):
                    here = pl.ds(pl.multiple_of(i * chunk + half * m, chunk), chunk)
                    p = direction[here, :]
                    p = p - alpha * image[here, :] + beta * p
                    direction[here, :] = p
                    rounded[1, here, :] = p.astype(BF16)
                    return carry

                lax.fori_loop(0, m // chunk, turn, 0)
                if half:
                    halo_to_sec_copy(1).start()
                else:
                    pl.when(has_next)(halo_to_sub_copy(1).start)
            store_direction = pltpu.make_async_copy(direction, direction_hbm, store_sem.at[0])
            store_direction.start()
        else:
            store_image = pltpu.make_async_copy(image, image_hbm, store_sem.at[1])
            store_image.start()
            (curvature,) = all_sum_get(it, 1)
            first_ref[...] = alpha
            turn_ref[...] = beta
            second_ref[...] = norm / curvature

    store_direction.wait()
    store_image.wait()
    pl.when(has_prev)(tell_sub.wait_send)
    tell_sec.wait_send()
    for it in range(ITERS):
        to_sub, to_sec = halo_copies(it)
        pl.when(has_next)(to_sub.wait_send)
        to_sec.wait_send()
        for copies in (back_copies(it), tip_copies(it)):
            pl.when(has_prev)(copies[0].wait_send)
            copies[1].wait_send()
        wait_all(part_sub.at[it, pl.ds(0, nsub - 1)], send_sem, it, CORNER_SUB)
        wait_all(part_sec.at[it, pl.ds(0, nsec - 1)], send_sem, it, CORNER_SEC)
        wait_all(coarse_all.at[it, pl.ds(0, share * (depth - 1))], send_sem, it, COARSE_SUB)
        wait_all(sum_first.at[it, pl.ds(0, len(first_steps))], send_sem, it, SUM_FIRST)
        wait_all(sum_second.at[it, pl.ds(0, len(second_steps))], send_sem, it, SUM_SECOND)


def shards(nsec, nsub, dual_load, flexibility, face_order, corner_index, coarse_inverse):
    _, _, _, m, cases = dual_load.shape
    rows = 4 * m
    nc = corner_index.shape[-1]
    share = cases // (nsub // 2)
    any_space = pl.BlockSpec(memory_space=pl.ANY)
    vmem = pl.BlockSpec(memory_space=pltpu.VMEM)
    it = ITERS
    scratch = [
        ((rows, rows), BF16),
        ((rows, rows), BF16),
        ((rows, rows), BF16),
        ((rows, LANES), jnp.int32),
        ((2 * m, cases), F32),
        ((it, 2 * m, cases), BF16),
        ((rows, cases), BF16),
        ((rows, cases), BF16),
        ((rows, cases), BF16),
        ((2 * m, cases), F32),
        ((2 * m, cases), F32),
        ((2 * m, cases), BF16),
        ((it, 2 * m, cases), BF16),
        ((it, m, cases), BF16),
        ((it, m, cases), BF16),
        ((it, m, cases), BF16),
        ((it, m, cases), BF16),
        ((it, nc, cases), F32),
        ((it, nc, cases), F32),
        ((it, nc, cases), F32),
        ((8, LANES), jnp.int32),
        ((8, LANES), jnp.int32),
        ((8, LANES), jnp.int32),
        ((rows, LANES), BF16),
        ((LANES, 2 * m), BF16),
        ((nc, 2 * m), BF16),
        ((m, LANES), BF16),
        ((m, LANES), BF16),
        ((nc, rows), BF16),
        ((2 * LANES, nsec * nc), F32),
        ((it, cases, LANES), BF16),
        ((it, nsub, share, LANES), BF16),
        ((it, share // 2, LANES), F32),
        ((it, nsec, share // 2, LANES), F32),
        ((it, share, 2 * LANES), BF16),
        ((it, cases, 2 * LANES), BF16),
        ((it, 8, LANES), F32),
        ((it, nsub // 2 * 2, 8, LANES), F32),
        ((it, 8, LANES), F32),
        ((it, nsec // 4 * 4, 8, LANES), F32),
    ]
    dma = pltpu.SemaphoreType.DMA
    out = jax.ShapeDtypeStruct((2 * m, cases), F32)
    row = jax.ShapeDtypeStruct((1, cases), F32)
    direction, image, first, turn, second = pl.pallas_call(
        functools.partial(kernel, nsec, nsub),
        out_shape=(out, out, row, row, row),
        in_specs=[any_space, any_space, vmem, vmem, any_space],
        out_specs=(any_space, any_space, vmem, vmem, vmem),
        scratch_shapes=[pltpu.VMEM(shape, dtype) for shape, dtype in scratch]
        + [dma((8,)), dma((2,)), dma((2,)), dma((2,)), dma((it, CHANNELS)), dma((it, CHANNELS))],
        compiler_params=pltpu.CompilerParams(
            collective_id=0, has_side_effects=True, vmem_limit_bytes=56 * 1024 * 1024
        ),
        cost_estimate=pl.CostEstimate(
            flops=16 * rows * rows * cases, bytes_accessed=2 * rows * rows, transcendentals=0
        ),
    )(
        dual_load.reshape(2 * m, cases),
        flexibility.reshape(rows, rows),
        face_order.reshape(1, rows),
        corner_index.reshape(1, nc),
        coarse_inverse,
    )
    direction, image = direction.reshape(dual_load.shape), image.reshape(dual_load.shape)
    first, turn, second = first.reshape(cases), turn.reshape(cases), second.reshape(cases)
    multiplier = first * dual_load + second * direction
    residual = direction - turn * dual_load - second * image
    return multiplier, residual


def solution(mesh):
    spec = P("sector", "sub", None, None, None)
    return jax.shard_map(
        functools.partial(shards, mesh.shape["sector"], mesh.shape["sub"]),
        mesh=mesh,
        in_specs=(
            spec,
            P("sector", "sub", None, None),
            P("sector", "sub", None),
            P("sector", "sub", None),
            P(),
        ),
        out_specs=(spec, spec),
        check_vma=False,
    )
```
